32 devices in a mesh: dp: 8 (over z, x), expert: 4 (over y, core).
Axes of the slice: x: 2, y: 2, z: 4, core: 2. Of those that a mesh axis runs over, the one named last changes fastest.
Arguments:
- tokens: bfloat16 [192, 6144], P('expert', 'dp'), may hold values from -6 to 6
- routing: int32 [192, 2], P('expert'), may hold values from 0 to 3, all different within a row; in each aligned block of 48 rows (0 to 47, 48 to 95, ...) at most 36 rows name the same one
- gates: int32 [192, 2], P('expert'), may hold values from 1 to 255
- w_gate: bfloat16 [4, 8192, 6144], P('expert', 'dp'), may hold values from -0.109375 to 0.109375
- w_up: bfloat16 [4, 8192, 6144], P('expert', 'dp'), may hold values from -0.078125 to 0.078125
- w_down: bfloat16 [4, 8192, 6144], P('expert', 'dp'), may hold values from -0.09375 to 0.09375
- cotangent: bfloat16 [192, 6144], P('expert', 'dp'), may hold values from -6 to 6
Outputs:
- mixed: bfloat16 [192, 6144], P('expert', 'dp')
- token_grad: bfloat16 [192, 6144], P('expert', 'dp')
- down_grad: bfloat16 [4, 8192, 6144], P('expert', 'dp')
The draws below stay inside these ranges and needn't reach their ends.
Inputs may be any that keep to these rules, and one draw needn't show every extreme that they name: `routing`: A token's two experts differ; in each aligned block of 48 tokens no expert is named by more than 36 choices, a bound that some block reaches.
All inputs are finite; a program needn't handle non-finite values.
Results may differ from the reference program's by a relative error of at most 0.0065.
Values may be sent and summed in bfloat16 or wider, within the bound.
A program may use at most 128 MiB of HBM per device.

```python
import math
import jax
import jax.numpy as jnp
import numpy as np
from jax import lax

D = 6144
FF = 8192
TOK_DEV = 48
EXPERTS = 4
CAP = 36
TOKENS = 192
N_EXPERT = 4


def touch_ends(entries, key, low, top_value):
    extent = entries.shape
    spot = [jax.random.randint(jax.random.fold_in(key, axis), (), 0, extent[axis]) for axis in range(len(extent))]
    entries = entries.at[tuple(spot)].set(low)
    longest = extent.index(max(extent))
    spot[longest] = (spot[longest] + 1) % extent[longest]
    return entries.at[tuple(spot)].set(top_value)


def strengthened(values, own_key, source, target, parts, factor):
    def block_of(position):
        return (jnp.arange(values.shape[position]) // (values.shape[position] // parts)).reshape((-1,) + (1,) * (values.ndim - 1 - position))

    near = jax.random.permutation(own_key, parts)[block_of(target)]
    second = (block_of(target) + parts // 2) % parts
    return jnp.where((block_of(source) == near) | (block_of(source) == second), factor * values, values)


def shard_levels(own_key, extent, shards, low, high):
    gain, own = 1.0, jax.random.fold_in(own_key, 6)
    for dim, parts in shards:
        draws = jnp.exp(jax.random.uniform(jax.random.fold_in(own, dim), (parts,), jnp.float32, low / len(shards), high / len(shards)))
        gain = gain * jnp.repeat(draws, extent[dim] // parts).reshape([-1 if axis == dim else 1 for axis in range(len(extent))])
    return gain


def assign_block(rng, own, number, rows, number_of, top, most, skew):
    order = jax.random.permutation(rng, number_of)
    crowded, usual = shares(number_of, rows * top, most, skew, True), shares(number_of, rows * top, most, skew, False)
    places = jnp.arange(number_of)

    def named(sizes, turn):
        used = int((sizes > 0).sum())
        fixed = max(1, used // 4)
        passed = fixed + (places - fixed + turn * (used - fixed)) % max(1, number_of - fixed)
        return jnp.zeros((number_of,), jnp.int32).at[order[jnp.where(places < fixed, places, passed)]].set(jnp.asarray(sizes, jnp.int32))

    sizes = jnp.where(number % 4 == 0, named(crowded, number // 4), named(usual, number - number // 4 - 1))
    mixed = jax.random.permutation(jax.random.fold_in(own, 3), number_of)
    donor, sink = mixed[0:number_of // 2 * 2:2], mixed[1:number_of // 2 * 2:2]
    room = jnp.minimum(sizes[donor] - 1, most - sizes[sink]) // 2
    room = jnp.where((donor == order[0]) | (sink == order[0]) | (sizes[sink] == 0), 0, jnp.maximum(room, 0))
    passed = jax.random.randint(jax.random.fold_in(own, 4), (number_of // 2,), 0, 1 << 20) % (room + 1)
    sizes = sizes.at[donor].add(-passed).at[sink].add(passed)
    items = jnp.searchsorted(jnp.cumsum(sizes), jnp.arange(rows * top), side="right").astype(jnp.int32)
    listing = items.reshape(top, rows).T
    listing = listing[jax.random.permutation(jax.random.fold_in(own, 1), rows)]
    turn = jax.random.randint(jax.random.fold_in(own, 2), (rows, 1), 0, top)
    return jnp.take_along_axis(listing, (jnp.arange(top)[None, :] + turn) % top, axis=1)


def shares(count, total, reach, lean, full):
    loads = [(1 << 20) // math.isqrt(grade ** lean) + 1 for grade in range(1, count + 1)]
    largest = reach if full else min(reach, max(-(-total // count), total * loads[0] // sum(loads)))
    least = 1 if total - largest >= count - 1 else 0
    given, spare = [largest] + [least] * (count - 1), total - largest - least * (count - 1)
    while spare > 0:
        movable = [i for i in range(1, count) if given[i] < largest] or [i for i in range(1, count) if given[i] < reach]
        mass, budget = sum([loads[i] for i in movable]), spare
        for i in movable:
            addition = min(reach - given[i], max(1, budget * loads[i] // mass), spare)
            given[i] = given[i] + addition
            spare = spare - addition
    return np.array(given)


def scatter_about(key, extent, spread, bound, cuts=(), kind=jnp.bfloat16):
    array = spread * jax.random.normal(key, extent, jnp.float32)
    if cuts:
        array = array * shard_levels(key, extent, cuts, -0.22, 0.18)
    return jnp.clip(array, -bound, bound).astype(kind)


def bell_draw_with(rng, extent, deviation, reach, split, heavy, held_as=jnp.bfloat16):
    values = deviation * jax.random.normal(rng, extent, jnp.float32)
    if split:
        values = values * shard_levels(rng, extent, split, -0.22, 0.18)
    return jnp.clip(strengthened(values, jax.random.fold_in(rng, 3), *heavy), -reach, reach).astype(held_as)


def setup_inputs(seed: int = 0) -> dict:
    streams_of = jax.random.split(jax.random.key(seed), 8)
    tokens = scatter_about(streams_of[0], (TOKENS, D), 1.0, 6.0, ((0, 4), (1, 8)))
    routing_keys = jax.random.split(jax.random.fold_in(streams_of[1], 1), TOKENS // TOK_DEV)
    routing_turns = jax.random.permutation(jax.random.fold_in(streams_of[1], 3), TOKENS // TOK_DEV)
    routing = jax.vmap(lambda own, number: assign_block(jax.random.fold_in(streams_of[1], 2), own, number, TOK_DEV, EXPERTS, 2, CAP, 2))(routing_keys, routing_turns).reshape((TOKENS, 2))
    gates = touch_ends(jax.random.randint(streams_of[2], (TOKENS, 2), 1, 256), jax.random.fold_in(streams_of[2], 1), 1, 255).astype(jnp.int32)
    w_gate = bell_draw_with(streams_of[3], (EXPERTS, FF, D), D ** -0.5, 0.109375, ((0, 4), (1, 8)), (1, 2, 8, 2.0))
    w_up = scatter_about(streams_of[4], (EXPERTS, FF, D), D ** -0.5, 0.078125, ((0, 4), (1, 8)))
    w_down = bell_draw_with(streams_of[5], (EXPERTS, FF, D), FF ** -0.5, 0.09375, ((0, 4), (1, 8)), (1, 2, 8, 2.0))
    cotangent = scatter_about(streams_of[6], (TOKENS, D), 1.0, 6.0, ((0, 4), (1, 8)))
    return {"tokens": tokens, "routing": routing, "gates": gates, "w_gate": w_gate, "w_up": w_up, "w_down": w_down, "cotangent": cotangent}


def reference(tokens, routing, gates, w_gate, w_up, w_down, cotangent):
    pair_ids = routing.reshape(N_EXPERT, 2 * TOK_DEV)
    expert_ids = jnp.arange(EXPERTS, dtype=jnp.int32)
    onehot = (pair_ids[:, :, None] == expert_ids[None, None, :]).astype(jnp.int32)
    earlier = jnp.cumsum(onehot, axis=1) - onehot
    slot_rank = jnp.sum(earlier * onehot, axis=2)
    block_base = (jnp.arange(N_EXPERT, dtype=jnp.int32) * CAP)[:, None]
    row_index = (block_base + slot_rank).astype(jnp.int32).reshape(TOKENS, 2)
    token_ids = jnp.broadcast_to(jnp.arange(TOKENS, dtype=jnp.int32)[:, None], (TOKENS, 2))
    scale = gates.astype(jnp.float32) / 256.0
    source = jnp.zeros((EXPERTS, N_EXPERT * CAP), jnp.int32).at[routing, row_index].set(token_ids)
    factor = jnp.zeros((EXPERTS, N_EXPERT * CAP), jnp.float32).at[routing, row_index].set(scale)
    filled = jnp.zeros((EXPERTS, N_EXPERT * CAP), jnp.float32).at[routing, row_index].set(1.0)
    dims = (((1,), (1,)), ((), ()))

    def one_expert(operands):
        gate_mat, up_mat, down_mat, src_ids, fac, fil = operands
        live = fil[:, None] > 0.5
        rows_in = jnp.where(live, tokens[src_ids], jnp.zeros((), jnp.bfloat16))
        scaled = (fac[:, None] * cotangent[src_ids].astype(jnp.float32)).astype(jnp.bfloat16)
        grads_in = jnp.where(live, scaled, jnp.zeros((), jnp.bfloat16))
        pre_gate = lax.dot_general(rows_in, gate_mat, dims, preferred_element_type=jnp.float32)
        pre_up = lax.dot_general(rows_in, up_mat, dims, preferred_element_type=jnp.float32)
        sigmoid_gate = jax.nn.sigmoid(pre_gate)
        swish = pre_gate * sigmoid_gate
        hidden = (swish * pre_up).astype(jnp.bfloat16)
        expert_out = jnp.dot(hidden, down_mat, preferred_element_type=jnp.float32).astype(jnp.bfloat16)
        hidden_grad = lax.dot_general(grads_in, down_mat, dims, preferred_element_type=jnp.float32)
        gate_grad = (hidden_grad * pre_up * sigmoid_gate * (1.0 + pre_gate * (1.0 - sigmoid_gate))).astype(jnp.bfloat16)
        up_grad = (hidden_grad * swish).astype(jnp.bfloat16)
        down_part = lax.dot_general(hidden, grads_in, (((0,), (0,)), ((), ())), preferred_element_type=jnp.float32).astype(jnp.bfloat16)
        back_sum = jnp.dot(gate_grad, gate_mat, preferred_element_type=jnp.float32) + jnp.dot(up_grad, up_mat, preferred_element_type=jnp.float32)
        return expert_out, back_sum.astype(jnp.bfloat16), down_part

    outs_all, backs_all, down_grad = lax.map(one_expert, (w_gate, w_up, w_down, source, factor, filled))
    picked = outs_all[routing, row_index].astype(jnp.float32)
    mixed = jnp.sum(scale[:, :, None] * picked, axis=1).astype(jnp.bfloat16)
    token_grad = jnp.sum(backs_all[routing, row_index].astype(jnp.float32), axis=1).astype(jnp.bfloat16)
    return mixed, token_grad, down_grad
```

```python
import jax
import jax.numpy as jnp
import jax.experimental.pallas as pl
from jax.experimental.pallas import tpu as pltpu
from jax import lax
from jax.sharding import PartitionSpec as P


def slot_tables(routing, gates, experts, capacity):
    pair_ids = routing.reshape(-1)
    expert_ids = lax.iota(jnp.int32, experts)
    onehot = (pair_ids[:, None] == expert_ids[None, :]).astype(jnp.int32)
    earlier = jnp.cumsum(onehot, axis=0) - onehot
    slot_rank = jnp.sum(earlier * onehot, axis=1)
    targets = (pair_ids * capacity + slot_rank).reshape(routing.shape)
    slot_ids = lax.iota(jnp.int32, experts * capacity)
    matches = slot_ids[:, None, None] == targets[None, :, :]
    placing = jnp.sum(matches.astype(jnp.float32), axis=2)
    weighting = jnp.sum(
        jnp.where(matches, gates[None, :, :].astype(jnp.float32) / 256.0, 0.0), axis=2
    )
    return (placing.astype(jnp.bfloat16), weighting.astype(jnp.bfloat16))


def per_device(tokens, routing, gates, w_gate, w_up, w_down, cotangent):
    experts = lax.axis_size("expert")
    capacity = 3 * tokens.shape[0] // experts
    placing, weighting = slot_tables(routing, gates, experts, capacity)
    gate_mat = w_gate[0]
    up_mat = w_up[0]
    down_mat = w_down[0]
    send_rows = jnp.dot(placing, tokens, preferred_element_type=jnp.float32).astype(jnp.bfloat16)
    send_grads = jnp.dot(weighting, cotangent, preferred_element_type=jnp.float32).astype(
        jnp.bfloat16
    )
    send_rows = send_rows.reshape(experts, capacity, -1)
    send_grads = send_grads.reshape(experts, capacity, -1)
    part_rows, part_grads = (
        lax.all_to_all(send_rows, "expert", split_axis=0, concat_axis=0, tiled=True),
        lax.all_to_all(send_grads, "expert", split_axis=0, concat_axis=0, tiled=True),
    )
    rows_in, grads_in = (
        lax.all_gather(part_rows, "dp", axis=2, tiled=True),
        lax.all_gather(part_grads, "dp", axis=2, tiled=True),
    )
    width = rows_in.shape[2]
    rows_in = rows_in.reshape(-1, width)
    grads_in = grads_in.reshape(-1, width)
    row_count = rows_in.shape[0]
    dims = (((1,), (1,)), ((), ()))
    across = (((0,), (1,)), ((), ()))
    pre_gate = lax.dot_general(rows_in, gate_mat, dims, preferred_element_type=jnp.float32)
    pre_up = lax.dot_general(rows_in, up_mat, dims, preferred_element_type=jnp.float32)
    sigmoid_gate = jax.nn.sigmoid(pre_gate)
    swish = pre_gate * sigmoid_gate
    hidden = (swish * pre_up).astype(jnp.bfloat16)
    hidden_grad = lax.dot_general(grads_in, down_mat, dims, preferred_element_type=jnp.float32)
    gate_grad = (
        hidden_grad * pre_up * sigmoid_gate * (1.0 + pre_gate * (1.0 - sigmoid_gate))
    ).astype(jnp.bfloat16)
    up_grad = (hidden_grad * swish).astype(jnp.bfloat16)
    down_grad = lax.dot_general(
        hidden, grads_in, (((0,), (0,)), ((), ())), preferred_element_type=jnp.float32
    )
    down_grad = down_grad.astype(jnp.bfloat16)[None]
    inward = lax.dot_general(gate_mat, gate_grad, across, preferred_element_type=jnp.float32)
    summed = lax.psum_scatter(
        jnp.concatenate(
            [
                lax.dot_general(down_mat, hidden, across, preferred_element_type=jnp.float32),
                inward
                + lax.dot_general(up_mat, up_grad, across, preferred_element_type=jnp.float32),
            ],
            axis=1,
        ),
        "dp",
        scatter_dimension=0,
        tiled=True,
    )
    out_summed = summed[:, :row_count]
    in_summed = summed[:, row_count:]
    expert_out = out_summed.T.astype(jnp.bfloat16).reshape(experts, capacity, -1)
    expert_back = in_summed.T.astype(jnp.bfloat16).reshape(experts, capacity, -1)
    back_out, back_grad = (
        lax.all_to_all(expert_out, "expert", split_axis=0, concat_axis=0, tiled=True),
        lax.all_to_all(expert_back, "expert", split_axis=0, concat_axis=0, tiled=True),
    )
    back_out = back_out.reshape(experts * capacity, -1)
    back_grad = back_grad.reshape(experts * capacity, -1)
    collect = (((0,), (0,)), ((), ()))
    mixed = lax.dot_general(
        weighting, back_out, collect, preferred_element_type=jnp.float32
    ).astype(jnp.bfloat16)
    token_grad = lax.dot_general(
        placing, back_grad, collect, preferred_element_type=jnp.float32
    ).astype(jnp.bfloat16)
    return (mixed, token_grad, down_grad)


MESH = pl.DeviceIdType.MESH
PARTS = 3
ORDERS = (
    ("zh", "zl", "x", "y", "core"),
    ("zh", "y", "zl", "x", "core"),
    ("zh", "x", "y", "zl", "core"),
)
STEPS = 5


def own_bits():
    dp, expert = lax.axis_index("dp"), lax.axis_index("expert")
    own = {
        "zh": dp // 4,
        "zl": (dp // 2) % 2,
        "x": dp % 2,
        "y": expert // 2,
        "core": expert % 2,
    }
    return {name: (bit, 1 - bit) for name, bit in own.items()}


def place(bits, flipped):
    at = {name: pair[1 if name in flipped else 0] for name, pair in bits.items()}
    return at["zh"] * 4 + at["zl"] * 2 + at["x"], at["y"] * 2 + at["core"]


def partner(bits, name):
    dp, expert = place(bits, (name,))
    return {"dp": dp, "expert": expert}


def flips(order, slot):
    return tuple(order[step] for step in range(STEPS) if slot >> step & 1)


def greet(others):
    barrier = pltpu.get_barrier_semaphore()
    for other in others:
        pl.semaphore_signal(barrier, inc=1, device_id=other, device_id_type=MESH)
    pl.semaphore_wait(barrier, len(others))


def gather_kernel(mine, meta, out, metas, slots, sends, recvs, meta_sends, meta_recvs):
    rows, width = mine.shape
    part_rows = rows // PARTS
    bits = own_bits()
    dp, expert = place(bits, ())
    row_of = [(("core",)), (("y",)), ("y", "core")]
    peers = []
    for names in row_of:
        peers.append({"dp": dp, "expert": place(bits, names)[1]})
    others = [partner(bits, name) for name in ("zh", "zl", "x", "y", "core")] + [peers[2]]
    greet(others)

    def copy(part, step):
        count = 1 << step
        return pltpu.make_async_remote_copy(
            src_ref=slots.at[part, pl.ds(0, count)],
            dst_ref=slots.at[part, pl.ds(count, count)],
            send_sem=sends.at[part, step],
            recv_sem=recvs.at[part, step],
            device_id=partner(bits, ORDERS[part][step]),
            device_id_type=MESH,
        )

    def settle(part, first, count):
        for slot in range(first, first + count):
            at_dp, at_expert = place(bits, flips(ORDERS[part], slot))
            row = pl.multiple_of(at_expert * rows + part * part_rows, 16)
            column = pl.multiple_of(at_dp * width, 128)
            out[pl.ds(row, part_rows), pl.ds(column, width)] = slots[part, slot]

    for part in range(PARTS):
        slots[part, 0] = mine[part * part_rows:(part + 1) * part_rows, :]
        copy(part, 0).start()
    meta_copies = []
    for i, peer in enumerate(peers):
        meta_copies.append(
            pltpu.make_async_remote_copy(
                src_ref=meta,
                dst_ref=metas.at[i + 1],
                send_sem=meta_sends.at[i],
                recv_sem=meta_recvs.at[i],
                device_id=peer,
                device_id_type=MESH,
            )
        )
        meta_copies[-1].start()
    metas[0] = meta[...]
    for part in range(PARTS):
        settle(part, 0, 1)
    for step in range(STEPS):
        for part in range(PARTS):
            copy(part, step).wait_recv()
            if step + 1 < STEPS:
                copy(part, step + 1).start()
            else:
                settle(part, 1 << step, 1 << step)
        if step + 1 < STEPS:
            for part in range(PARTS):
                settle(part, 1 << step, 1 << step)
    for each in meta_copies:
        each.wait()
    for step in range(STEPS):
        for part in range(PARTS):
            copy(part, step).wait_send()


def scatter_kernel(partial, out, slots, inbox, sends, recvs):
    rows, width = out.shape
    part_rows = rows // PARTS
    bits = own_bits()
    greet([partner(bits, name) for name in ("zh", "zl", "x", "y", "core")])

    def copy(part, step):
        count = 1 << step
        return pltpu.make_async_remote_copy(
            src_ref=slots.at[part, pl.ds(count, count)],
            dst_ref=inbox.at[part, pl.ds(count, count)],
            send_sem=sends.at[part, step],
            recv_sem=recvs.at[part, step],
            device_id=partner(bits, ORDERS[part][step]),
            device_id_type=MESH,
        )

    def pick(part, first, count):
        for slot in range(first, first + count):
            at_dp, at_expert = place(bits, flips(ORDERS[part], slot))
            row = pl.multiple_of(at_expert * rows + part * part_rows, 16)
            column = pl.multiple_of(at_dp * width, 128)
            slots[part, slot] = partial[pl.ds(row, part_rows), pl.ds(column, width)]

    def add(part, step, first, count):
        for slot in range(first, first + count):
            total = slots[part, slot].astype(jnp.float32) + inbox[
                part, (1 << step) + slot
            ].astype(jnp.float32)
            slots[part, slot] = total.astype(jnp.bfloat16)

    top = STEPS - 1
    for part in range(PARTS):
        pick(part, 1 << top, 1 << top)
        copy(part, top).start()
    for part in range(PARTS):
        pick(part, 0, 1 << top)
    for step in range(top, 0, -1):
        half = 1 << (step - 1)
        for part in range(PARTS):
            copy(part, step).wait_recv()
            add(part, step, half, half)
            copy(part, step - 1).start()
        for part in range(PARTS):
            add(part, step, 0, half)
    for part in range(PARTS):
        copy(part, 0).wait_recv()
        total = slots[part, 0].astype(jnp.float32) + inbox[part, 1].astype(jnp.float32)
        out[part * part_rows:(part + 1) * part_rows, :] = total.astype(jnp.bfloat16)
    for step in range(STEPS):
        for part in range(PARTS):
            copy(part, step).wait_send()


def vmem():
    return pl.BlockSpec(memory_space=pltpu.VMEM)


def gather_all(mine, meta):
    rows, width = mine.shape
    part_rows = rows // PARTS
    dma = pltpu.SemaphoreType.DMA
    return pl.pallas_call(
        gather_kernel,
        out_shape=(
            jax.ShapeDtypeStruct((4 * rows, 8 * width), jnp.bfloat16),
            jax.ShapeDtypeStruct((4,) + meta.shape, jnp.bfloat16),
        ),
        in_specs=[vmem(), vmem()],
        out_specs=(vmem(), vmem()),
        scratch_shapes=[
            pltpu.VMEM((PARTS, 1 << STEPS, part_rows, width), jnp.bfloat16),
            dma((PARTS, STEPS)),
            dma((PARTS, STEPS)),
            dma((3,)),
            dma((3,)),
        ],
        compiler_params=pltpu.CompilerParams(
            collective_id=0, has_side_effects=True, vmem_limit_bytes=32 << 20
        ),
    )(mine, meta)


def scatter_sum(partial, rows, width):
    part_rows = rows // PARTS
    dma = pltpu.SemaphoreType.DMA
    return pl.pallas_call(
        scatter_kernel,
        out_shape=jax.ShapeDtypeStruct((rows, width), jnp.bfloat16),
        in_specs=[vmem()],
        out_specs=vmem(),
        scratch_shapes=[
            pltpu.VMEM((PARTS, 1 << STEPS, part_rows, width), jnp.bfloat16),
            pltpu.VMEM((PARTS, 1 << STEPS, part_rows, width), jnp.bfloat16),
            dma((PARTS, STEPS)),
            dma((PARTS, STEPS)),
        ],
        compiler_params=pltpu.CompilerParams(
            collective_id=1, has_side_effects=True, vmem_limit_bytes=32 << 20
        ),
    )(partial)


def per_device_cube(tokens, routing, gates, w_gate, w_up, w_down, cotangent):
    experts = lax.axis_size("expert")
    own = lax.axis_index("expert")
    count, width = tokens.shape
    capacity = 3 * count // experts
    row_count = experts * capacity
    gate_mat, up_mat, down_mat = w_gate[0], w_up[0], w_down[0]
    meta = jnp.concatenate([routing.T, gates.T], axis=0).astype(jnp.bfloat16)
    meta = jnp.pad(meta, ((0, 12), (0, 128 - count)))
    everything, metas = gather_all(jnp.concatenate([tokens, cotangent], axis=0), meta)
    block = lax.iota(jnp.int32, experts)
    metas = jnp.take(metas, block ^ own, axis=0)[:, :4, :count].astype(jnp.float32)
    named = metas[:, :2] == own.astype(jnp.float32)
    hit = jnp.sum(named.astype(jnp.float32), axis=1)
    weight = jnp.sum(jnp.where(named, metas[:, 2:], 0.0), axis=1) / 256.0
    place_id = lax.iota(jnp.int32, count)
    before = (place_id[:, None] < place_id[None, :]).astype(jnp.bfloat16)
    rank = jnp.dot(hit.astype(jnp.bfloat16), before, preferred_element_type=jnp.float32)
    target = rank.astype(jnp.int32) + block[:, None] * capacity
    matches = (lax.iota(jnp.int32, row_count)[:, None, None] == target[None]) & (hit > 0.5)[None]
    placing = matches.astype(jnp.bfloat16)
    weighting = jnp.where(matches, weight[None], 0.0).astype(jnp.bfloat16)
    none = jnp.zeros_like(placing)

    def joined(first, second):
        upper = jnp.concatenate([first, none], axis=2).reshape(row_count, -1)
        lower = jnp.concatenate([none, second], axis=2).reshape(row_count, -1)
        return jnp.concatenate([upper, lower], axis=0)

    into, back = joined(placing, weighting), joined(weighting, placing)
    both = jnp.dot(into, everything, preferred_element_type=jnp.float32).astype(jnp.bfloat16)
    rows_in, grads_in = both[:row_count], both[row_count:]
    dims = (((1,), (1,)), ((), ()))
    across = (((0,), (1,)), ((), ()))
    pre_gate = lax.dot_general(rows_in, gate_mat, dims, preferred_element_type=jnp.float32)
    pre_up = lax.dot_general(rows_in, up_mat, dims, preferred_element_type=jnp.float32)
    sigmoid_gate = jax.nn.sigmoid(pre_gate)
    swish = pre_gate * sigmoid_gate
    hidden = (swish * pre_up).astype(jnp.bfloat16)
    hidden_grad = lax.dot_general(grads_in, down_mat, dims, preferred_element_type=jnp.float32)
    gate_grad = (
        hidden_grad * pre_up * sigmoid_gate * (1.0 + pre_gate * (1.0 - sigmoid_gate))
    ).astype(jnp.bfloat16)
    up_grad = (hidden_grad * swish).astype(jnp.bfloat16)
    down_grad = lax.dot_general(
        hidden, grads_in, (((0,), (0,)), ((), ())), preferred_element_type=jnp.float32
    )
    down_grad = down_grad.astype(jnp.bfloat16)[None]
    outward = lax.dot_general(down_mat, hidden, across, preferred_element_type=jnp.float32)
    inward = lax.dot_general(
        gate_mat, gate_grad, across, preferred_element_type=jnp.float32
    ) + lax.dot_general(up_mat, up_grad, across, preferred_element_type=jnp.float32)
    sums = jnp.concatenate(
        [outward.astype(jnp.bfloat16), inward.astype(jnp.bfloat16)], axis=1
    )
    partial = lax.dot_general(
        back, sums, across, preferred_element_type=jnp.float32
    ).astype(jnp.bfloat16)
    summed = scatter_sum(partial, 2 * count, width)
    return summed[:count], summed[count:], down_grad


def cube_fits(mesh, tokens):
    shape = (mesh.shape["dp"], mesh.shape["expert"])
    rows, width = tokens.shape[0] // shape[1], tokens.shape[1] // shape[0]
    return shape == (8, 4) and width % 128 == 0 and rows % 24 == 0 and rows <= 128


def solution(mesh):
    def program(tokens, *rest):
        body = per_device_cube if cube_fits(mesh, tokens) else per_device
        return on_mesh(mesh, body)(tokens, *rest)

    return program


def on_mesh(mesh, body):
    return jax.shard_map(
        body,
        mesh=mesh,
        in_specs=(
            P("expert", "dp"),
            P("expert", None),
            P("expert", None),
            P("expert", "dp", None),
            P("expert", "dp", None),
            P("expert", "dp", None),
            P("expert", "dp"),
        ),
        out_specs=(P("expert", "dp"), P("expert", "dp"), P("expert", "dp", None)),
        check_vma=False,
    )
```

```python
import jax
import jax.numpy as jnp
import jax.experimental.pallas as pl
from jax.experimental.pallas import tpu as pltpu
from jax import lax
from jax.sharding import PartitionSpec as P


def slot_tables(routing, gates, experts, capacity):
    pair_ids = routing.reshape(-1)
    expert_ids = lax.iota(jnp.int32, experts)
    onehot = (pair_ids[:, None] == expert_ids[None, :]).astype(jnp.int32)
    earlier = jnp.cumsum(onehot, axis=0) - onehot
    slot_rank = jnp.sum(earlier * onehot, axis=1)
    targets = (pair_ids * capacity + slot_rank).reshape(routing.shape)
    slot_ids = lax.iota(jnp.int32, experts * capacity)
    matches = slot_ids[:, None, None] == targets[None, :, :]
    placing = jnp.sum(matches.astype(jnp.float32), axis=2)
    weighting = jnp.sum(
        jnp.where(matches, gates[None, :, :].astype(jnp.float32) / 256.0, 0.0), axis=2
    )
    return (placing.astype(jnp.bfloat16), weighting.astype(jnp.bfloat16))


def per_device(tokens, routing, gates, w_gate, w_up, w_down, cotangent):
    experts = lax.axis_size("expert")
    capacity = 3 * tokens.shape[0] // experts
    placing, weighting = slot_tables(routing, gates, experts, capacity)
    gate_mat = w_gate[0]
    up_mat = w_up[0]
    down_mat = w_down[0]
    send_rows = jnp.dot(placing, tokens, preferred_element_type=jnp.float32).astype(jnp.bfloat16)
    send_grads = jnp.dot(weighting, cotangent, preferred_element_type=jnp.float32).astype(
        jnp.bfloat16
    )
    send_rows = send_rows.reshape(experts, capacity, -1)
    send_grads = send_grads.reshape(experts, capacity, -1)
    part_rows, part_grads = (
        lax.all_to_all(send_rows, "expert", split_axis=0, concat_axis=0, tiled=True),
        lax.all_to_all(send_grads, "expert", split_axis=0, concat_axis=0, tiled=True),
    )
    rows_in, grads_in = (
        lax.all_gather(part_rows, "dp", axis=2, tiled=True),
        lax.all_gather(part_grads, "dp", axis=2, tiled=True),
    )
    width = rows_in.shape[2]
    rows_in = rows_in.reshape(-1, width)
    grads_in = grads_in.reshape(-1, width)
    row_count = rows_in.shape[0]
    dims = (((1,), (1,)), ((), ()))
    across = (((0,), (1,)), ((), ()))
    pre_gate = lax.dot_general(rows_in, gate_mat, dims, preferred_element_type=jnp.float32)
    pre_up = lax.dot_general(rows_in, up_mat, dims, preferred_element_type=jnp.float32)
    sigmoid_gate = jax.nn.sigmoid(pre_gate)
    swish = pre_gate * sigmoid_gate
    hidden = (swish * pre_up).astype(jnp.bfloat16)
    hidden_grad = lax.dot_general(grads_in, down_mat, dims, preferred_element_type=jnp.float32)
    gate_grad = (
        hidden_grad * pre_up * sigmoid_gate * (1.0 + pre_gate * (1.0 - sigmoid_gate))
    ).astype(jnp.bfloat16)
    up_grad = (hidden_grad * swish).astype(jnp.bfloat16)
    down_grad = lax.dot_general(
        hidden, grads_in, (((0,), (0,)), ((), ())), preferred_element_type=jnp.float32
    )
    down_grad = down_grad.astype(jnp.bfloat16)[None]
    inward = lax.dot_general(gate_mat, gate_grad, across, preferred_element_type=jnp.float32)
    summed = lax.psum_scatter(
        jnp.concatenate(
            [
                lax.dot_general(down_mat, hidden, across, preferred_element_type=jnp.float32),
                inward
                + lax.dot_general(up_mat, up_grad, across, preferred_element_type=jnp.float32),
            ],
            axis=1,
        ),
        "dp",
        scatter_dimension=0,
        tiled=True,
    )
    out_summed = summed[:, :row_count]
    in_summed = summed[:, row_count:]
    expert_out = out_summed.T.astype(jnp.bfloat16).reshape(experts, capacity, -1)
    expert_back = in_summed.T.astype(jnp.bfloat16).reshape(experts, capacity, -1)
    back_out, back_grad = (
        lax.all_to_all(expert_out, "expert", split_axis=0, concat_axis=0, tiled=True),
        lax.all_to_all(expert_back, "expert", split_axis=0, concat_axis=0, tiled=True),
    )
    back_out = back_out.reshape(experts * capacity, -1)
    back_grad = back_grad.reshape(experts * capacity, -1)
    collect = (((0,), (0,)), ((), ()))
    mixed = lax.dot_general(
        weighting, back_out, collect, preferred_element_type=jnp.float32
    ).astype(jnp.bfloat16)
    token_grad = lax.dot_general(
        placing, back_grad, collect, preferred_element_type=jnp.float32
    ).astype(jnp.bfloat16)
    return (mixed, token_grad, down_grad)


MESH = pl.DeviceIdType.MESH
PARTS = 3
ORDERS = (
    ("zh", "zl", "x", "y", "core"),
    ("zh", "y", "zl", "x", "core"),
    ("zh", "x", "y", "zl", "core"),
)
STEPS = 5


def own_bits():
    dp, expert = lax.axis_index("dp"), lax.axis_index("expert")
    own = {
        "zh": dp // 4,
        "zl": (dp // 2) % 2,
        "x": dp % 2,
        "y": expert // 2,
        "core": expert % 2,
    }
    return {name: (bit, 1 - bit) for name, bit in own.items()}


def place(bits, flipped):
    at = {name: pair[1 if name in flipped else 0] for name, pair in bits.items()}
    return at["zh"] * 4 + at["zl"] * 2 + at["x"], at["y"] * 2 + at["core"]


def partner(bits, name):
    dp, expert = place(bits, (name,))
    return {"dp": dp, "expert": expert}


def flips(order, slot):
    return tuple(order[step] for step in range(STEPS) if slot >> step & 1)


def greet(others):
    barrier = pltpu.get_barrier_semaphore()
    for other in others:
        pl.semaphore_signal(barrier, inc=1, device_id=other, device_id_type=MESH)
    pl.semaphore_wait(barrier, len(others))


def gather_kernel(mine, meta, out, metas, slots, sends, recvs, meta_sends, meta_recvs):
    rows, width = mine.shape
    part_rows = rows // PARTS
    bits = own_bits()
    dp, expert = place(bits, ())
    row_of = [(("core",)), (("y",)), ("y", "core")]
    peers = []
    for names in row_of:
        peers.append({"dp": dp, "expert": place(bits, names)[1]})
    others = [partner(bits, name) for name in ("zh", "zl", "x", "y", "core")] + [peers[2]]
    greet(others)

    def copy(part, step):
        count = 1 << step
        return pltpu.make_async_remote_copy(
            src_ref=slots.at[part, pl.ds(0, count)],
            dst_ref=slots.at[part, pl.ds(count, count)],
            send_sem=sends.at[part, step],
            recv_sem=recvs.at[part, step],
            device_id=partner(bits, ORDERS[part][step]),
            device_id_type=MESH,
        )

    def settle(part, first, count):
        for slot in range(first, first + count):
            at_dp, at_expert = place(bits, flips(ORDERS[part], slot))
            row = pl.multiple_of(at_expert * rows + part * part_rows, 16)
            column = pl.multiple_of(at_dp * width, 128)
            out[pl.ds(row, part_rows), pl.ds(column, width)] = slots[part, slot]

    for part in range(PARTS):
        slots[part, 0] = mine[part * part_rows:(part + 1) * part_rows, :]
        copy(part, 0).start()
    meta_copies = []
    for i, peer in enumerate(peers):
        meta_copies.append(
            pltpu.make_async_remote_copy(
                src_ref=meta,
                dst_ref=metas.at[i + 1],
                send_sem=meta_sends.at[i],
                recv_sem=meta_recvs.at[i],
                device_id=peer,
                device_id_type=MESH,
            )
        )
        meta_copies[-1].start()
    metas[0] = meta[...]
    for part in range(PARTS):
        settle(part, 0, 1)
    for step in range(STEPS):
        for part in range(PARTS):
            copy(part, step).wait_recv()
            if step + 1 < STEPS:
                copy(part, step + 1).start()
            else:
                settle(part, 1 << step, 1 << step)
        if step + 1 < STEPS:
            for part in range(PARTS):
                settle(part, 1 << step, 1 << step)
    for each in meta_copies:
        each.wait()
    for step in range(STEPS):
        for part in range(PARTS):
            copy(part, step).wait_send()


def scatter_kernel(partial, out, slots, kept, inbox, sends, recvs):
    rows, width = out.shape
    part_rows = rows // PARTS
    bits = own_bits()
    greet([partner(bits, name) for name in ("zh", "zl", "x", "y", "core")])
    top = STEPS - 1

    def copy(part, step):
        count = 1 << step
        return pltpu.make_async_remote_copy(
            src_ref=slots.at[part, pl.ds(count, count)],
            dst_ref=inbox.at[part, pl.ds(count, count)],
            send_sem=sends.at[part, step],
            recv_sem=recvs.at[part, step],
            device_id=partner(bits, ORDERS[part][step]),
            device_id_type=MESH,
        )

    def block(part, slot):
        at_dp, at_expert = place(bits, flips(ORDERS[part], slot))
        row = pl.multiple_of(at_expert * rows + part * part_rows, 16)
        column = pl.multiple_of(at_dp * width, 128)
        return partial[pl.ds(row, part_rows), pl.ds(column, width)]

    def total(part, step, slot):
        if step == top:
            own = block(part, slot).astype(jnp.float32)
        else:
            own = kept[part, slot]
        return own + inbox[part, (1 << step) + slot].astype(jnp.float32)

    for part in range(PARTS):
        for slot in range(1 << top, 2 << top):
            slots[part, slot] = block(part, slot)
        copy(part, top).start()
    for step in range(top, 0, -1):
        half = 1 << (step - 1)
        for part in range(PARTS):
            copy(part, step).wait_recv()
            for slot in range(half, 2 * half):
                slots[part, slot] = total(part, step, slot).astype(jnp.bfloat16)
            copy(part, step - 1).start()
        for part in range(PARTS):
            for slot in range(half):
                kept[part, slot] = total(part, step, slot)
    for part in range(PARTS):
        copy(part, 0).wait_recv()
        out[part * part_rows:(part + 1) * part_rows, :] = total(part, 0, 0).astype(
            jnp.bfloat16
        )
    for step in range(STEPS):
        for part in range(PARTS):
            copy(part, step).wait_send()


def expert_kernel(into, back, everything, w_gate, w_up, w_down, partial, down_grad, both, sums):
    count = into.shape[0] // 2
    width = everything.shape[1]
    wide = width // 8
    step = pl.program_id(0)

    @pl.when(step == 0)
    def _():
        @pl.loop(0, 8)
        def _(i):
            at = pl.ds(pl.multiple_of(i * wide, wide), wide)
            placed = jnp.dot(into[...], everything[:, at], preferred_element_type=jnp.float32)
            both[:, at] = placed.astype(jnp.bfloat16)
            sums[:, at] = jnp.zeros((2 * count, wide), jnp.float32)

    dims = (((1,), (1,)), ((), ()))
    rows_in, grads_in = both[:count, :], both[count:, :]
    pre_gate = lax.dot_general(rows_in, w_gate[0], dims, preferred_element_type=jnp.float32)
    pre_up = lax.dot_general(rows_in, w_up[0], dims, preferred_element_type=jnp.float32)
    hidden_grad = lax.dot_general(grads_in, w_down[0], dims, preferred_element_type=jnp.float32)
    sigmoid_gate = jax.nn.sigmoid(pre_gate)
    swish = pre_gate * sigmoid_gate
    hidden = (swish * pre_up).astype(jnp.bfloat16)
    gate_grad = (
        hidden_grad * pre_up * sigmoid_gate * (1.0 + pre_gate * (1.0 - sigmoid_gate))
    ).astype(jnp.bfloat16)
    up_grad = (hidden_grad * swish).astype(jnp.bfloat16)
    turned = hidden.T

    @pl.loop(0, 8)
    def _(i):
        at = pl.ds(pl.multiple_of(i * wide, wide), wide)
        sums[:count, at] += jnp.dot(hidden, w_down[0, :, at], preferred_element_type=jnp.float32)
        sums[count:, at] += jnp.dot(
            gate_grad, w_gate[0, :, at], preferred_element_type=jnp.float32
        ) + jnp.dot(up_grad, w_up[0, :, at], preferred_element_type=jnp.float32)
        down_grad[0, :, at] = jnp.dot(
            turned, both[count:, at], preferred_element_type=jnp.float32
        ).astype(jnp.bfloat16)

    @pl.when(step == pl.num_programs(0) - 1)
    def _():
        @pl.loop(0, 8)
        def _(i):
            at = pl.ds(pl.multiple_of(i * wide, wide), wide)
            partial[:, at] = jnp.dot(
                back[...], sums[:, at].astype(jnp.bfloat16), preferred_element_type=jnp.float32
            ).astype(jnp.bfloat16)


def run_expert(into, back, everything, w_gate, w_up, w_down):
    units, width = w_gate.shape[1:]
    tile = 256 if units % 256 == 0 else units

    def whole(array):
        return pl.BlockSpec(array.shape, lambda i: (0, 0), pipeline_mode=pl.Buffered(1))

    def tiled():
        return pl.BlockSpec((1, tile, width), lambda i: (0, i, 0))

    return pl.pallas_call(
        expert_kernel,
        grid=(units // tile,),
        out_shape=(
            jax.ShapeDtypeStruct(everything.shape, jnp.bfloat16),
            jax.ShapeDtypeStruct(w_gate.shape, jnp.bfloat16),
        ),
        in_specs=[whole(into), whole(back), whole(everything), tiled(), tiled(), tiled()],
        out_specs=(whole(everything), tiled()),
        scratch_shapes=[
            pltpu.VMEM((into.shape[0], width), jnp.bfloat16),
            pltpu.VMEM((into.shape[0], width), jnp.float32),
        ],
        compiler_params=pltpu.CompilerParams(vmem_limit_bytes=58 << 20),
    )(into, back, everything, w_gate, w_up, w_down)


def vmem():
    return pl.BlockSpec(memory_space=pltpu.VMEM)


def gather_all(mine, meta):
    rows, width = mine.shape
    part_rows = rows // PARTS
    dma = pltpu.SemaphoreType.DMA
    return pl.pallas_call(
        gather_kernel,
        out_shape=(
            jax.ShapeDtypeStruct((4 * rows, 8 * width), jnp.bfloat16),
            jax.ShapeDtypeStruct((4,) + meta.shape, jnp.bfloat16),
        ),
        in_specs=[vmem(), vmem()],
        out_specs=(vmem(), vmem()),
        scratch_shapes=[
            pltpu.VMEM((PARTS, 1 << STEPS, part_rows, width), jnp.bfloat16),
            dma((PARTS, STEPS)),
            dma((PARTS, STEPS)),
            dma((3,)),
            dma((3,)),
        ],
        compiler_params=pltpu.CompilerParams(
            collective_id=0, has_side_effects=True, vmem_limit_bytes=32 << 20
        ),
    )(mine, meta)


def scatter_sum(partial, rows, width):
    part_rows = rows // PARTS
    dma = pltpu.SemaphoreType.DMA
    return pl.pallas_call(
        scatter_kernel,
        out_shape=jax.ShapeDtypeStruct((rows, width), jnp.bfloat16),
        in_specs=[vmem()],
        out_specs=vmem(),
        scratch_shapes=[
            pltpu.VMEM((PARTS, 1 << STEPS, part_rows, width), jnp.bfloat16),
            pltpu.VMEM((PARTS, 1 << (STEPS - 2), part_rows, width), jnp.float32),
            pltpu.VMEM((PARTS, 1 << STEPS, part_rows, width), jnp.bfloat16),
            dma((PARTS, STEPS)),
            dma((PARTS, STEPS)),
        ],
        compiler_params=pltpu.CompilerParams(
            collective_id=1, has_side_effects=True, vmem_limit_bytes=32 << 20
        ),
    )(partial)


def per_device_cube(tokens, routing, gates, w_gate, w_up, w_down, cotangent):
    experts = lax.axis_size("expert")
    own = lax.axis_index("expert")
    count, width = tokens.shape
    capacity = 3 * count // experts
    row_count = experts * capacity
    meta = jnp.concatenate([routing.T, gates.T], axis=0).astype(jnp.bfloat16)
    meta = jnp.pad(meta, ((0, 12), (0, 128 - count)))
    everything, metas = gather_all(jnp.concatenate([tokens, cotangent], axis=0), meta)
    block = lax.iota(jnp.int32, experts)
    metas = jnp.take(metas, block ^ own, axis=0)[:, :4, :count].astype(jnp.float32)
    named = metas[:, :2] == own.astype(jnp.float32)
    hit = jnp.sum(named.astype(jnp.float32), axis=1)
    weight = jnp.sum(jnp.where(named, metas[:, 2:], 0.0), axis=1) / 256.0
    place_id = lax.iota(jnp.int32, count)
    before = (place_id[:, None] < place_id[None, :]).astype(jnp.bfloat16)
    rank = jnp.dot(hit.astype(jnp.bfloat16), before, preferred_element_type=jnp.float32)
    target = rank.astype(jnp.int32) + block[:, None] * capacity
    matches = (lax.iota(jnp.int32, row_count)[:, None, None] == target[None]) & (hit > 0.5)[None]
    placing = matches.astype(jnp.bfloat16)
    weighting = jnp.where(matches, weight[None], 0.0).astype(jnp.bfloat16)
    none = jnp.zeros_like(placing)

    def joined(first, second):
        upper = jnp.concatenate([first, none], axis=2).reshape(row_count, -1)
        lower = jnp.concatenate([none, second], axis=2).reshape(row_count, -1)
        return jnp.concatenate([upper, lower], axis=0)

    into, back = joined(placing, weighting), joined(weighting, placing)
    partial, down_grad = run_expert(into, back.T, everything, w_gate, w_up, w_down)
    summed = scatter_sum(partial, 2 * count, width)
    return summed[:count], summed[count:], down_grad


def cube_fits(mesh, tokens):
    shape = (mesh.shape["dp"], mesh.shape["expert"])
    rows, width = tokens.shape[0] // shape[1], tokens.shape[1] // shape[0]
    return shape == (8, 4) and width % 128 == 0 and rows % 24 == 0 and rows <= 128


def solution(mesh):
    def program(tokens, *rest):
        body = per_device_cube if cube_fits(mesh, tokens) else per_device
        return on_mesh(mesh, body)(tokens, *rest)

    return program


def on_mesh(mesh, body):
    return jax.shard_map(
        body,
        mesh=mesh,
        in_specs=(
            P("expert", "dp"),
            P("expert", None),
            P("expert", None),
            P("expert", "dp", None),
            P("expert", "dp", None),
            P("expert", "dp", None),
            P("expert", "dp"),
        ),
        out_specs=(P("expert", "dp"), P("expert", "dp"), P("expert", "dp", None)),
        check_vma=False,
    )
```

```python
import jax
import jax.numpy as jnp
import jax.experimental.pallas as pl
from jax.experimental.pallas import tpu as pltpu
from jax import lax
from jax.sharding import PartitionSpec as P


def slot_tables(routing, gates, experts, capacity):
    pair_ids = routing.reshape(-1)
    expert_ids = lax.iota(jnp.int32, experts)
    onehot = (pair_ids[:, None] == expert_ids[None, :]).astype(jnp.int32)
    earlier = jnp.cumsum(onehot, axis=0) - onehot
    slot_rank = jnp.sum(earlier * onehot, axis=1)
    targets = (pair_ids * capacity + slot_rank).reshape(routing.shape)
    slot_ids = lax.iota(jnp.int32, experts * capacity)
    matches = slot_ids[:, None, None] == targets[None, :, :]
    placing = jnp.sum(matches.astype(jnp.float32), axis=2)
    weighting = jnp.sum(
        jnp.where(matches, gates[None, :, :].astype(jnp.float32) / 256.0, 0.0), axis=2
    )
    return (placing.astype(jnp.bfloat16), weighting.astype(jnp.bfloat16))


def per_device(tokens, routing, gates, w_gate, w_up, w_down, cotangent):
    experts = lax.axis_size("expert")
    capacity = 3 * tokens.shape[0] // experts
    placing, weighting = slot_tables(routing, gates, experts, capacity)
    gate_mat = w_gate[0]
    up_mat = w_up[0]
    down_mat = w_down[0]
    send_rows = jnp.dot(placing, tokens, preferred_element_type=jnp.float32).astype(jnp.bfloat16)
    send_grads = jnp.dot(weighting, cotangent, preferred_element_type=jnp.float32).astype(
        jnp.bfloat16
    )
    send_rows = send_rows.reshape(experts, capacity, -1)
    send_grads = send_grads.reshape(experts, capacity, -1)
    part_rows, part_grads = (
        lax.all_to_all(send_rows, "expert", split_axis=0, concat_axis=0, tiled=True),
        lax.all_to_all(send_grads, "expert", split_axis=0, concat_axis=0, tiled=True),
    )
    rows_in, grads_in = (
        lax.all_gather(part_rows, "dp", axis=2, tiled=True),
        lax.all_gather(part_grads, "dp", axis=2, tiled=True),
    )
    width = rows_in.shape[2]
    rows_in = rows_in.reshape(-1, width)
    grads_in = grads_in.reshape(-1, width)
    row_count = rows_in.shape[0]
    dims = (((1,), (1,)), ((), ()))
    across = (((0,), (1,)), ((), ()))
    pre_gate = lax.dot_general(rows_in, gate_mat, dims, preferred_element_type=jnp.float32)
    pre_up = lax.dot_general(rows_in, up_mat, dims, preferred_element_type=jnp.float32)
    sigmoid_gate = jax.nn.sigmoid(pre_gate)
    swish = pre_gate * sigmoid_gate
    hidden = (swish * pre_up).astype(jnp.bfloat16)
    hidden_grad = lax.dot_general(grads_in, down_mat, dims, preferred_element_type=jnp.float32)
    gate_grad = (
        hidden_grad * pre_up * sigmoid_gate * (1.0 + pre_gate * (1.0 - sigmoid_gate))
    ).astype(jnp.bfloat16)
    up_grad = (hidden_grad * swish).astype(jnp.bfloat16)
    down_grad = lax.dot_general(
        hidden, grads_in, (((0,), (0,)), ((), ())), preferred_element_type=jnp.float32
    )
    down_grad = down_grad.astype(jnp.bfloat16)[None]
    inward = lax.dot_general(gate_mat, gate_grad, across, preferred_element_type=jnp.float32)
    summed = lax.psum_scatter(
        jnp.concatenate(
            [
                lax.dot_general(down_mat, hidden, across, preferred_element_type=jnp.float32),
                inward
                + lax.dot_general(up_mat, up_grad, across, preferred_element_type=jnp.float32),
            ],
            axis=1,
        ),
        "dp",
        scatter_dimension=0,
        tiled=True,
    )
    out_summed = summed[:, :row_count]
    in_summed = summed[:, row_count:]
    expert_out = out_summed.T.astype(jnp.bfloat16).reshape(experts, capacity, -1)
    expert_back = in_summed.T.astype(jnp.bfloat16).reshape(experts, capacity, -1)
    back_out, back_grad = (
        lax.all_to_all(expert_out, "expert", split_axis=0, concat_axis=0, tiled=True),
        lax.all_to_all(expert_back, "expert", split_axis=0, concat_axis=0, tiled=True),
    )
    back_out = back_out.reshape(experts * capacity, -1)
    back_grad = back_grad.reshape(experts * capacity, -1)
    collect = (((0,), (0,)), ((), ()))
    mixed = lax.dot_general(
        weighting, back_out, collect, preferred_element_type=jnp.float32
    ).astype(jnp.bfloat16)
    token_grad = lax.dot_general(
        placing, back_grad, collect, preferred_element_type=jnp.float32
    ).astype(jnp.bfloat16)
    return (mixed, token_grad, down_grad)


MESH = pl.DeviceIdType.MESH
PARTS = 3
ORDERS = (
    ("zh", "zl", "x", "y", "core"),
    ("zh", "y", "zl", "x", "core"),
    ("zh", "x", "y", "zl", "core"),
)
STEPS = 5


def own_bits():
    dp, expert = lax.axis_index("dp"), lax.axis_index("expert")
    own = {
        "zh": dp // 4,
        "zl": (dp // 2) % 2,
        "x": dp % 2,
        "y": expert // 2,
        "core": expert % 2,
    }
    return {name: (bit, 1 - bit) for name, bit in own.items()}


def place(bits, flipped):
    at = {name: pair[1 if name in flipped else 0] for name, pair in bits.items()}
    return at["zh"] * 4 + at["zl"] * 2 + at["x"], at["y"] * 2 + at["core"]


def partner(bits, name):
    dp, expert = place(bits, (name,))
    return {"dp": dp, "expert": expert}


def flips(order, slot):
    return tuple(order[step] for step in range(STEPS) if slot >> step & 1)


def greet(others):
    barrier = pltpu.get_barrier_semaphore()
    for other in others:
        pl.semaphore_signal(barrier, inc=1, device_id=other, device_id_type=MESH)
    pl.semaphore_wait(barrier, len(others))


def gather_kernel(mine, meta, out, metas, slots, sends, recvs, meta_sends, meta_recvs):
    rows, width = mine.shape
    part_rows = rows // PARTS
    bits = own_bits()
    dp, expert = place(bits, ())
    row_of = [(("core",)), (("y",)), ("y", "core")]
    peers = []
    for names in row_of:
        peers.append({"dp": dp, "expert": place(bits, names)[1]})
    others = [partner(bits, name) for name in ("zh", "zl", "x", "y", "core")] + [peers[2]]
    greet(others)

    def copy(part, step):
        count = 1 << step
        return pltpu.make_async_remote_copy(
            src_ref=slots.at[part, pl.ds(0, count)],
            dst_ref=slots.at[part, pl.ds(count, count)],
            send_sem=sends.at[part, step],
            recv_sem=recvs.at[part, step],
            device_id=partner(bits, ORDERS[part][step]),
            device_id_type=MESH,
        )

    def settle(part, first, count):
        for slot in range(first, first + count):
            at_dp, at_expert = place(bits, flips(ORDERS[part], slot))
            row = pl.multiple_of(at_expert * rows + part * part_rows, 16)
            column = pl.multiple_of(at_dp * width, 128)
            out[pl.ds(row, part_rows), pl.ds(column, width)] = slots[part, slot]

    for part in range(PARTS):
        slots[part, 0] = mine[part * part_rows:(part + 1) * part_rows, :]
        copy(part, 0).start()
    meta_copies = []
    for i, peer in enumerate(peers):
        meta_copies.append(
            pltpu.make_async_remote_copy(
                src_ref=meta,
                dst_ref=metas.at[i + 1],
                send_sem=meta_sends.at[i],
                recv_sem=meta_recvs.at[i],
                device_id=peer,
                device_id_type=MESH,
            )
        )
        meta_copies[-1].start()
    metas[0] = meta[...]
    for part in range(PARTS):
        settle(part, 0, 1)
    for step in range(STEPS):
        for part in range(PARTS):
            copy(part, step).wait_recv()
            if step + 1 < STEPS:
                copy(part, step + 1).start()
            else:
                settle(part, 1 << step, 1 << step)
        if step + 1 < STEPS:
            for part in range(PARTS):
                settle(part, 1 << step, 1 << step)
    for each in meta_copies:
        each.wait()
    for step in range(STEPS):
        for part in range(PARTS):
            copy(part, step).wait_send()


def scatter_kernel(partial, out, slots, kept, inbox, sends, recvs):
    rows, width = out.shape
    part_rows = rows // PARTS
    bits = own_bits()
    greet([partner(bits, name) for name in ("zh", "zl", "x", "y", "core")])
    top = STEPS - 1

    def copy(part, step):
        count = 1 << step
        return pltpu.make_async_remote_copy(
            src_ref=slots.at[part, pl.ds(count, count)],
            dst_ref=inbox.at[part, pl.ds(count, count)],
            send_sem=sends.at[part, step],
            recv_sem=recvs.at[part, step],
            device_id=partner(bits, ORDERS[part][step]),
            device_id_type=MESH,
        )

    def block(part, slot):
        at_dp, at_expert = place(bits, flips(ORDERS[part], slot))
        row = pl.multiple_of(at_expert * rows + part * part_rows, 16)
        column = pl.multiple_of(at_dp * width, 128)
        return partial[pl.ds(row, part_rows), pl.ds(column, width)]

    def total(part, step, slot):
        if step == top:
            own = block(part, slot).astype(jnp.float32)
        else:
            own = kept[part, slot]
        return own + inbox[part, (1 << step) + slot].astype(jnp.float32)

    for part in range(PARTS):
        for slot in range(1 << top, 2 << top):
            slots[part, slot] = block(part, slot)
        copy(part, top).start()
    for step in range(top, 0, -1):
        half = 1 << (step - 1)
        for part in range(PARTS):
            copy(part, step).wait_recv()
            for slot in range(half, 2 * half):
                slots[part, slot] = total(part, step, slot).astype(jnp.bfloat16)
            copy(part, step - 1).start()
        for part in range(PARTS):
            for slot in range(half):
                kept[part, slot] = total(part, step, slot)
    for part in range(PARTS):
        copy(part, 0).wait_recv()
        out[part * part_rows:(part + 1) * part_rows, :] = total(part, 0, 0).astype(
            jnp.bfloat16
        )
    for step in range(STEPS):
        for part in range(PARTS):
            copy(part, step).wait_send()


def expert_kernel(into, back, everything, w_gate, w_up, w_down, partial, down_grad, both, sums):
    count = into.shape[0] // 2
    width = everything.shape[1]
    wide = width // 4
    step = pl.program_id(0)

    @pl.when(step == 0)
    def _():
        @pl.loop(0, 4)
        def _(i):
            at = pl.ds(pl.multiple_of(i * wide, wide), wide)
            placed = jnp.dot(into[...], everything[:, at], preferred_element_type=jnp.float32)
            both[:, at] = placed.astype(jnp.bfloat16)
            sums[:, at] = jnp.zeros((2 * count, wide), jnp.float32)

    dims = (((1,), (1,)), ((), ()))
    rows_in, grads_in = both[:count, :], both[count:, :]
    pre_gate = lax.dot_general(w_gate[0], rows_in, dims, preferred_element_type=jnp.float32)
    pre_up = lax.dot_general(w_up[0], rows_in, dims, preferred_element_type=jnp.float32)
    hidden_grad = lax.dot_general(w_down[0], grads_in, dims, preferred_element_type=jnp.float32)
    sigmoid_gate = jax.nn.sigmoid(pre_gate)
    swish = pre_gate * sigmoid_gate
    turned = (swish * pre_up).astype(jnp.bfloat16)
    gate_grad = (
        hidden_grad * pre_up * sigmoid_gate * (1.0 + pre_gate * (1.0 - sigmoid_gate))
    ).astype(jnp.bfloat16).T
    up_grad = (hidden_grad * swish).astype(jnp.bfloat16).T
    hidden = turned.T

    @pl.loop(0, 4)
    def _(i):
        at = pl.ds(pl.multiple_of(i * wide, wide), wide)
        sums[:count, at] += jnp.dot(hidden, w_down[0, :, at], preferred_element_type=jnp.float32)
        sums[count:, at] += jnp.dot(
            gate_grad, w_gate[0, :, at], preferred_element_type=jnp.float32
        ) + jnp.dot(up_grad, w_up[0, :, at], preferred_element_type=jnp.float32)
        down_grad[0, :, at] = jnp.dot(
            turned, both[count:, at], preferred_element_type=jnp.float32
        ).astype(jnp.bfloat16)

    @pl.when(step == pl.num_programs(0) - 1)
    def _():
        @pl.loop(0, 4)
        def _(i):
            at = pl.ds(pl.multiple_of(i * wide, wide), wide)
            partial[:, at] = jnp.dot(
                back[...], sums[:, at].astype(jnp.bfloat16), preferred_element_type=jnp.float32
            ).astype(jnp.bfloat16)


def run_expert(into, back, everything, w_gate, w_up, w_down):
    units, width = w_gate.shape[1:]
    tile = 256 if units % 256 == 0 else units

    def whole(array):
        return pl.BlockSpec(array.shape, lambda i: (0, 0), pipeline_mode=pl.Buffered(1))

    def tiled():
        return pl.BlockSpec((1, tile, width), lambda i: (0, i, 0))

    return pl.pallas_call(
        expert_kernel,
        grid=(units // tile,),
        out_shape=(
            jax.ShapeDtypeStruct(everything.shape, jnp.bfloat16),
            jax.ShapeDtypeStruct(w_gate.shape, jnp.bfloat16),
        ),
        in_specs=[whole(into), whole(back), whole(everything), tiled(), tiled(), tiled()],
        out_specs=(whole(everything), tiled()),
        scratch_shapes=[
            pltpu.VMEM((into.shape[0], width), jnp.bfloat16),
            pltpu.VMEM((into.shape[0], width), jnp.float32),
        ],
        compiler_params=pltpu.CompilerParams(vmem_limit_bytes=58 << 20),
    )(into, back, everything, w_gate, w_up, w_down)


def vmem():
    return pl.BlockSpec(memory_space=pltpu.VMEM)


def gather_all(mine, meta):
    rows, width = mine.shape
    part_rows = rows // PARTS
    dma = pltpu.SemaphoreType.DMA
    return pl.pallas_call(
        gather_kernel,
        out_shape=(
            jax.ShapeDtypeStruct((4 * rows, 8 * width), jnp.bfloat16),
            jax.ShapeDtypeStruct((4,) + meta.shape, jnp.bfloat16),
        ),
        in_specs=[vmem(), vmem()],
        out_specs=(vmem(), vmem()),
        scratch_shapes=[
            pltpu.VMEM((PARTS, 1 << STEPS, part_rows, width), jnp.bfloat16),
            dma((PARTS, STEPS)),
            dma((PARTS, STEPS)),
            dma((3,)),
            dma((3,)),
        ],
        compiler_params=pltpu.CompilerParams(
            collective_id=0, has_side_effects=True, vmem_limit_bytes=32 << 20
        ),
    )(mine, meta)


def scatter_sum(partial, rows, width):
    part_rows = rows // PARTS
    dma = pltpu.SemaphoreType.DMA
    return pl.pallas_call(
        scatter_kernel,
        out_shape=jax.ShapeDtypeStruct((rows, width), jnp.bfloat16),
        in_specs=[vmem()],
        out_specs=vmem(),
        scratch_shapes=[
            pltpu.VMEM((PARTS, 1 << STEPS, part_rows, width), jnp.bfloat16),
            pltpu.VMEM((PARTS, 1 << (STEPS - 2), part_rows, width), jnp.float32),
            pltpu.VMEM((PARTS, 1 << STEPS, part_rows, width), jnp.bfloat16),
            dma((PARTS, STEPS)),
            dma((PARTS, STEPS)),
        ],
        compiler_params=pltpu.CompilerParams(
            collective_id=1, has_side_effects=True, vmem_limit_bytes=32 << 20
        ),
    )(partial)


def per_device_cube(tokens, routing, gates, w_gate, w_up, w_down, cotangent):
    experts = lax.axis_size("expert")
    own = lax.axis_index("expert")
    count, width = tokens.shape
    capacity = 3 * count // experts
    row_count = experts * capacity
    meta = jnp.concatenate([routing.T, gates.T], axis=0).astype(jnp.bfloat16)
    meta = jnp.pad(meta, ((0, 12), (0, 128 - count)))
    everything, metas = gather_all(jnp.concatenate([tokens, cotangent], axis=0), meta)
    block = lax.iota(jnp.int32, experts)
    metas = jnp.take(metas, block ^ own, axis=0)[:, :4, :count].astype(jnp.float32)
    named = metas[:, :2] == own.astype(jnp.float32)
    hit = jnp.sum(named.astype(jnp.float32), axis=1)
    weight = jnp.sum(jnp.where(named, metas[:, 2:], 0.0), axis=1) / 256.0
    place_id = lax.iota(jnp.int32, count)
    before = (place_id[:, None] < place_id[None, :]).astype(jnp.bfloat16)
    rank = jnp.dot(hit.astype(jnp.bfloat16), before, preferred_element_type=jnp.float32)
    target = rank.astype(jnp.int32) + block[:, None] * capacity
    matches = (lax.iota(jnp.int32, row_count)[:, None, None] == target[None]) & (hit > 0.5)[None]
    placing = matches.astype(jnp.bfloat16)
    weighting = jnp.where(matches, weight[None], 0.0).astype(jnp.bfloat16)
    none = jnp.zeros_like(placing)

    def joined(first, second):
        upper = jnp.concatenate([first, none], axis=2).reshape(row_count, -1)
        lower = jnp.concatenate([none, second], axis=2).reshape(row_count, -1)
        return jnp.concatenate([upper, lower], axis=0)

    into, back = joined(placing, weighting), joined(weighting, placing)
    partial, down_grad = run_expert(into, back.T, everything, w_gate, w_up, w_down)
    summed = scatter_sum(partial, 2 * count, width)
    return summed[:count], summed[count:], down_grad


def cube_fits(mesh, tokens):
    shape = (mesh.shape["dp"], mesh.shape["expert"])
    rows, width = tokens.shape[0] // shape[1], tokens.shape[1] // shape[0]
    return shape == (8, 4) and width % 128 == 0 and rows % 24 == 0 and rows <= 128


def solution(mesh):
    def program(tokens, *rest):
        body = per_device_cube if cube_fits(mesh, tokens) else per_device
        return on_mesh(mesh, body)(tokens, *rest)

    return program


def on_mesh(mesh, body):
    return jax.shard_map(
        body,
        mesh=mesh,
        in_specs=(
            P("expert", "dp"),
            P("expert", None),
            P("expert", None),
            P("expert", "dp", None),
            P("expert", "dp", None),
            P("expert", "dp", None),
            P("expert", "dp"),
        ),
        out_specs=(P("expert", "dp"), P("expert", "dp"), P("expert", "dp", None)),
        check_vma=False,
    )
```
